32 devices in a mesh: prompt: 8 (over y, x, core), resp: 4 (over z).
Axes of the slice: x: 2, y: 2, z: 4, core: 2. Of those that a mesh axis runs over, the one named last changes fastest.
Arguments:
- queries: bfloat16 [4096, 2048], P(('prompt', 'resp'))
- resp_keys: bfloat16 [4096, 2048], P(('prompt', 'resp')), may hold values from -6 to 6
- resp_values: bfloat16 [4096, 2048], P(('prompt', 'resp')), may hold values from -6 to 6
- grad_out: bfloat16 [4096, 2048], P(('prompt', 'resp')), may hold values from -3 to 3
- prefix_keys: bfloat16 [2048, 2048], P(('prompt', 'resp'))
- prefix_values: bfloat16 [2048, 2048], P(('prompt', 'resp')), may hold values from -6 to 6
- block_mask: int32 [32, 2], P(('prompt', 'resp')), may hold values from 0 to 1, as said below
- lengths: int32 [32], P(('prompt', 'resp')), may hold values from 1 to 128, as said below
Outputs:
- attended: bfloat16 [4096, 2048], P(('prompt', 'resp'))
- grad_queries: bfloat16 [4096, 2048], P(('prompt', 'resp'))
- grad_resp_keys: bfloat16 [4096, 2048], P(('prompt', 'resp'))
- grad_resp_values: bfloat16 [4096, 2048], P(('prompt', 'resp'))
- grad_prefix_keys: bfloat16 [2048, 2048], P(('prompt', 'resp'))
- grad_prefix_values: bfloat16 [2048, 2048], P(('prompt', 'resp'))
The draws below stay inside these ranges and needn't reach their ends.
Inputs may be any that keep to these rules, and one draw needn't show every extreme that they name: `block_mask`: column 0 is 1 for every response. `lengths`: the last response of every prompt has length 128.
All inputs are finite; a program needn't handle non-finite values.
Results may differ from the reference program's by a relative error of at most 0.019.
Values may be sent and summed in bfloat16 or wider, within the bound.
A program may use at most 128 MiB of HBM per device.

```python
import jax
import jax.numpy as jnp
from jax import lax

H = 16
HD = 128
F = 2048
BLK = 128
RLEN = 128
PROMPTS = 8
RESPS = 4
PREF = 256
NBLK = 2
ROWS = 4096


def base_keys(key):
    return jax.random.normal(jax.random.fold_in(key, 11), (PROMPTS * PREF, F), jnp.float32)


def draw_prefix_keys(key, part):
    shared = base_keys(key)
    return shared.astype(jnp.bfloat16)


def draw_queries(key, part):
    key = jax.random.fold_in(key, 5)
    drawn = 2.0 * jax.random.normal(key, (ROWS, F), jnp.float32)
    return drawn.astype(jnp.bfloat16)


def draw_block_mask(key, part):
    key = jax.random.fold_in(key, 7)
    random_bits = jax.random.randint(key, (PROMPTS * RESPS, NBLK), 0, 2, dtype=jnp.int32)
    first_block = (jnp.arange(NBLK, dtype=jnp.int32) == 0)[None, :]
    return jnp.where(first_block, 1, random_bits).astype(jnp.int32)


def draw_lengths(key, part):
    key = jax.random.fold_in(key, 9)
    position = jnp.arange(PROMPTS * RESPS, dtype=jnp.int32)
    slot = position % RESPS
    ceiling = RLEN // 3 + (RLEN - RLEN // 3) * slot // max(RESPS - 1, 1)
    lowest = jnp.maximum(ceiling // 2, 1)
    random_units = jax.random.randint(key, (PROMPTS * RESPS,), 0, 1 << 20, dtype=jnp.int32)
    drawn = lowest + random_units % (ceiling - lowest + 1)
    return jnp.where(slot == RESPS - 1, RLEN, drawn).astype(jnp.int32)


def level_of(key, extent, pieces, smallest, top_value):
    factor_of, own = 1.0, jax.random.fold_in(key, 6)
    for axis_at, blocks in pieces:
        heights = jnp.exp(jax.random.uniform(jax.random.fold_in(own, axis_at), (blocks,), jnp.float32, smallest / len(pieces), top_value / len(pieces)))
        factor_of = factor_of * jnp.repeat(heights, extent[axis_at] // blocks).reshape([-1 if axis == axis_at else 1 for axis in range(len(extent))])
    return factor_of


def bell_draw(own_key, shape, scale, most, split=(), kind=jnp.bfloat16):
    level = level_of(own_key, shape, split, -0.22, 0.18) if split else 1.0
    array = jax.random.normal(own_key, shape, jnp.float32) * scale * level
    return jnp.minimum(jnp.maximum(array, -most), most).astype(kind)


def setup_inputs(seed: int = 0) -> dict:
    streams_of = jax.random.split(jax.random.key(seed), 9)
    return {
        "queries": draw_queries(jax.random.fold_in(streams_of[8], 71), 0),
        "resp_keys": bell_draw(streams_of[1], (ROWS, F), 1.0, 6.0, ((0, 32),)),
        "resp_values": bell_draw(streams_of[2], (ROWS, F), 1.0, 6.0, ((0, 32),)),
        "grad_out": bell_draw(streams_of[3], (ROWS, F), 0.5, 3.0, ((0, 32),)),
        "prefix_keys": draw_prefix_keys(jax.random.fold_in(streams_of[8], 71), 0),
        "prefix_values": bell_draw(streams_of[5], (PROMPTS * PREF, F), 1.0, 6.0, ((0, 32),)),
        "block_mask": draw_block_mask(jax.random.fold_in(streams_of[8], 71), 0),
        "lengths": draw_lengths(jax.random.fold_in(streams_of[8], 71), 0),
    }


def respond(query, own_keys, own_values, cotangent, pref_keys, pref_values, mask_row, length):
    scaling = 1.0 / (HD ** 0.5)
    keys = jnp.concatenate([pref_keys, own_keys], 0).astype(jnp.float32).reshape(PREF + RLEN, H, HD)
    values = jnp.concatenate([pref_values, own_values], 0).astype(jnp.float32).reshape(PREF + RLEN, H, HD)
    query3 = query.astype(jnp.float32).reshape(RLEN, H, HD)
    positions = jnp.arange(PREF, dtype=jnp.int32) // BLK
    table = jnp.arange(NBLK, dtype=jnp.int32)
    pref_visible = jnp.sum(jnp.where(positions[:, None] == table[None, :], mask_row[None, :], 0), axis=1) > 0
    row_index = jnp.arange(RLEN, dtype=jnp.int32)
    own_visible = row_index[None, :] <= row_index[:, None]
    visible = jnp.concatenate([jnp.broadcast_to(pref_visible[None, :], (RLEN, PREF)), own_visible], 1)
    scores = jnp.einsum('shd,khd->hsk', query3, keys) * scaling
    scores = jnp.where(visible[None], scores, -jnp.inf)
    highest = jnp.max(scores, axis=2, keepdims=True)
    expsum = jnp.sum(jnp.exp(scores - highest), axis=2, keepdims=True)
    log_mass = highest + jnp.log(expsum)
    probs = jnp.exp(scores - log_mass)
    weights = lax.optimization_barrier(probs.astype(jnp.bfloat16)).astype(jnp.float32)
    attended = jnp.einsum('hsk,khd->shd', weights, values).reshape(RLEN, F).astype(jnp.bfloat16)
    valid = (row_index < length).astype(jnp.float32)
    grads3 = (cotangent.astype(jnp.float32) * valid[:, None]).reshape(RLEN, H, HD)
    out3 = attended.astype(jnp.float32).reshape(RLEN, H, HD)
    delta = jnp.einsum('shd,shd->hs', grads3, out3)
    dprob = jnp.einsum('shd,khd->hsk', grads3, values)
    dscore = lax.optimization_barrier((probs * (dprob - delta[..., None])).astype(jnp.bfloat16)).astype(jnp.float32)
    grad_query = (jnp.einsum('hsk,khd->shd', dscore, keys) * scaling).reshape(RLEN, F).astype(jnp.bfloat16)
    grad_key = (jnp.einsum('hsk,shd->khd', dscore, query3) * scaling).reshape(PREF + RLEN, F)
    grad_value = jnp.einsum('hsk,shd->khd', weights, grads3).reshape(PREF + RLEN, F)
    return (attended, grad_query, grad_key[PREF:].astype(jnp.bfloat16), grad_value[PREF:].astype(jnp.bfloat16),
            grad_key[:PREF].astype(jnp.bfloat16), grad_value[:PREF].astype(jnp.bfloat16))


def reference(queries, resp_keys, resp_values, grad_out, prefix_keys, prefix_values, block_mask, lengths):
    query_all = queries.reshape(PROMPTS, RESPS, RLEN, F)
    key_all = resp_keys.reshape(PROMPTS, RESPS, RLEN, F)
    value_all = resp_values.reshape(PROMPTS, RESPS, RLEN, F)
    grad_all = grad_out.reshape(PROMPTS, RESPS, RLEN, F)
    pkey_all = prefix_keys.reshape(PROMPTS, PREF, F)
    pvalue_all = prefix_values.reshape(PROMPTS, PREF, F)
    mask_all = block_mask.reshape(PROMPTS, RESPS, NBLK)
    length_all = lengths.reshape(PROMPTS, RESPS)

    def one_prompt(items):
        query_p, key_p, value_p, grad_p, pkey, pvalue, mask_p, length_p = items

        def one_response(inner):
            query_r, key_r, value_r, grad_r, mask_r, length_r = inner
            return respond(query_r, key_r, value_r, grad_r, pkey, pvalue, mask_r, length_r)

        outputs = lax.map(one_response, (query_p, key_p, value_p, grad_p, mask_p, length_p))
        pref_gk = jnp.sum(outputs[4].astype(jnp.float32), axis=0).astype(jnp.bfloat16)
        pref_gv = jnp.sum(outputs[5].astype(jnp.float32), axis=0).astype(jnp.bfloat16)
        return outputs[0], outputs[1], outputs[2], outputs[3], pref_gk, pref_gv

    result = lax.map(one_prompt, (query_all, key_all, value_all, grad_all, pkey_all, pvalue_all, mask_all, length_all))
    return (result[0].reshape(ROWS, F), result[1].reshape(ROWS, F), result[2].reshape(ROWS, F),
            result[3].reshape(ROWS, F), result[4].reshape(PROMPTS * PREF, F), result[5].reshape(PROMPTS * PREF, F))
```

```python
import functools

import jax
import jax.numpy as jnp
from jax import lax
from jax.experimental import pallas as pl
from jax.experimental.pallas import tpu as pltpu
from jax.sharding import PartitionSpec as P

HD = 128
BLK = 128
WIDTH = 256
AHEAD = 2
MESH = pl.DeviceIdType.MESH

GATHER_RIGHT, GATHER_LEFT, SUM_RIGHT, SUM_LEFT = 0, 1, 2, 3


def kernel(
    groups,
    mask_ref,
    length_ref,
    q_hbm,
    k_hbm,
    v_hbm,
    g_hbm,
    pk_hbm,
    pv_hbm,
    att_hbm,
    gq_hbm,
    gk_hbm,
    gv_hbm,
    gpk_hbm,
    gpv_hbm,
    kv,
    ins,
    outs,
    term,
    from_left,
    from_right,
    summed,
    total,
    visible,
    send_sem,
    recv_sem,
    prefix_sem,
    in_sem,
    out_sem,
    sum_sem,
):
    me = lax.axis_index("resp")
    chunks, _, _, span, width = kv.shape
    rows = ins.shape[2]
    prefix = groups * span
    last = groups - 1
    has_left = me > 0
    has_right = me < last

    def columns(c):
        return pl.ds(pl.multiple_of(c * width, width), width)

    def prefix_copy(c, which):
        source = (pk_hbm, pv_hbm)[which]
        return pltpu.make_async_copy(
            source.at[:, columns(c)], kv.at[c, me, which], prefix_sem.at[c, which]
        )

    def in_copy(c, which):
        source = (q_hbm, k_hbm, v_hbm, g_hbm)[which]
        return pltpu.make_async_copy(
            source.at[:, columns(c)], ins.at[which, c], in_sem.at[c, which]
        )

    def out_copy(c, which):
        target = (att_hbm, gq_hbm, gk_hbm, gv_hbm)[which]
        return pltpu.make_async_copy(
            outs.at[which, c], target.at[:, columns(c)], out_sem.at[c, which]
        )

    def sum_copy(c, which):
        target = (gpk_hbm, gpv_hbm)[which]
        return pltpu.make_async_copy(
            summed.at[c, which], target.at[:, columns(c)], sum_sem.at[c, which]
        )

    def remote(kind, c, slot):
        buffer = (kv, kv, from_left, from_right)[kind]
        to = me + 1 if kind in (GATHER_RIGHT, SUM_RIGHT) else me - 1
        return pltpu.make_async_remote_copy(
            src_ref=buffer.at[c, slot],
            dst_ref=buffer.at[c, slot],
            send_sem=send_sem.at[kind, c, slot],
            recv_sem=recv_sem.at[kind, c, slot],
            device_id={"resp": to},
            device_id_type=MESH,
        )

    def send_own(c):
        for which in range(2):
            prefix_copy(c, which).wait()

        @pl.when(has_right)
        def _():
            remote(GATHER_RIGHT, c, me).start()

        @pl.when(has_left)
        def _():
            remote(GATHER_LEFT, c, me).start()

    def start_prefix(c, carry):
        for which in range(2):
            prefix_copy(c, which).start()
        return carry

    def start_ins(c, carry):
        for which in range(4):
            in_copy(c, which).start()
        return carry

    lax.fori_loop(0, chunks, start_prefix, 0)
    barrier = pltpu.get_barrier_semaphore()

    @pl.when(has_left)
    def _():
        pl.semaphore_signal(barrier, inc=1, device_id={"resp": me - 1}, device_id_type=MESH)

    @pl.when(has_right)
    def _():
        pl.semaphore_signal(barrier, inc=1, device_id={"resp": me + 1}, device_id_type=MESH)

    @pl.when(has_left & has_right)
    def _():
        pl.semaphore_wait(barrier, 2)

    @pl.when(jnp.logical_not(has_left & has_right))
    def _():
        pl.semaphore_wait(barrier, 1)

    for c in range(AHEAD):
        send_own(c)
    lax.fori_loop(0, chunks, start_ins, 0)

    key_at = lax.broadcasted_iota(jnp.int32, (rows, prefix + rows), 1)
    row_at = lax.broadcasted_iota(jnp.int32, (rows, prefix + rows), 0)
    seen = jnp.where(key_at - prefix <= row_at, 1, 0)
    for block in range(prefix // BLK):
        inside = (key_at >= block * BLK) & (key_at < (block + 1) * BLK)
        seen = jnp.where(inside, mask_ref[0, block], seen)
    visible[...] = seen
    scaling = 1.0 / HD**0.5

    def gather(c):
        for hop in range(1, groups):

            @pl.when(me - hop >= 0)
            def _():
                remote(GATHER_RIGHT, c, me - hop).wait_recv()

                @pl.when(has_right)
                def _():
                    remote(GATHER_RIGHT, c, me - hop).start()

            @pl.when(me + hop <= last)
            def _():
                remote(GATHER_LEFT, c, me + hop).wait_recv()

                @pl.when(has_left)
                def _():
                    remote(GATHER_LEFT, c, me + hop).start()

    def attend(c):
        for which in range(4):
            in_copy(c, which).wait()
        valid = lax.broadcasted_iota(jnp.int32, (rows, HD), 0) < length_ref[0]
        for head in range(width // HD):
            at = slice(head * HD, (head + 1) * HD)
            query = ins[0, c, :, at]
            keys = jnp.concatenate(
                [kv[c, :, 0, :, at].reshape(prefix, HD), ins[1, c, :, at]], axis=0
            )
            values = jnp.concatenate(
                [kv[c, :, 1, :, at].reshape(prefix, HD), ins[2, c, :, at]], axis=0
            )
            grad32 = jnp.where(valid, ins[3, c, :, at].astype(jnp.float32), 0.0)
            grad = grad32.astype(jnp.bfloat16)
            across = (((1,), (1,)), ((), ()))
            down = (((0,), (0,)), ((), ()))
            scores = (
                lax.dot_general(query, keys, across, preferred_element_type=jnp.float32) * scaling
            )
            scores = jnp.where(visible[...] > 0, scores, -jnp.inf)
            powers = jnp.exp(scores - jnp.max(scores, axis=1, keepdims=True))
            probs = powers * (1.0 / jnp.sum(powers, axis=1, keepdims=True))
            weights = probs.astype(jnp.bfloat16)
            attended = jnp.dot(weights, values, preferred_element_type=jnp.float32).astype(
                jnp.bfloat16
            )
            outs[0, c, :, at] = attended
            delta = jnp.sum(grad32 * attended.astype(jnp.float32), axis=1, keepdims=True)
            dprob = lax.dot_general(grad, values, across, preferred_element_type=jnp.float32)
            dscore = (probs * (dprob - delta)).astype(jnp.bfloat16)
            grad_query = jnp.dot(dscore, keys, preferred_element_type=jnp.float32) * scaling
            outs[1, c, :, at] = grad_query.astype(jnp.bfloat16)
            grad_key = (
                lax.dot_general(dscore, query, down, preferred_element_type=jnp.float32) * scaling
            ).astype(jnp.bfloat16)
            grad_value = lax.dot_general(
                weights, grad, down, preferred_element_type=jnp.float32
            ).astype(jnp.bfloat16)
            term[c, :, 0, :, at] = grad_key[:prefix].reshape(groups, span, HD)
            term[c, :, 1, :, at] = grad_value[:prefix].reshape(groups, span, HD)
            outs[2, c, :, at] = grad_key[prefix:]
            outs[3, c, :, at] = grad_value[prefix:]
        for which in range(4):
            out_copy(c, which).start()

    def relay(kind, buffer, c, slot, receives):
        @pl.when(receives)
        def _():
            remote(kind, c, slot).wait_recv()
            buffer[c, slot] = (
                buffer[c, slot].astype(jnp.float32) + term[c, slot].astype(jnp.float32)
            ).astype(jnp.bfloat16)

        @pl.when(jnp.logical_not(receives))
        def _():
            buffer[c, slot] = term[c, slot]

        remote(kind, c, slot).start()

    def finish(c):
        total[...] = term[c, me].astype(jnp.float32)

        @pl.when(has_left)
        def _():
            remote(SUM_RIGHT, c, me).wait_recv()
            total[...] += from_left[c, me].astype(jnp.float32)

        @pl.when(has_right)
        def _():
            remote(SUM_LEFT, c, me).wait_recv()
            total[...] += from_right[c, me].astype(jnp.float32)

        summed[c] = total[...].astype(jnp.bfloat16)
        for which in range(2):
            sum_copy(c, which).start()
        for hop in range(groups):

            @pl.when((me - hop >= 0) & has_right)
            def _():
                remote(GATHER_RIGHT, c, me - hop).wait_send()

            @pl.when((me + hop <= last) & has_left)
            def _():
                remote(GATHER_LEFT, c, me + hop).wait_send()

            if hop > 0:

                @pl.when(me + hop <= last)
                def _():
                    remote(SUM_RIGHT, c, me + hop).wait_send()

                @pl.when(me - hop >= 0)
                def _():
                    remote(SUM_LEFT, c, me - hop).wait_send()

        for which in range(4):
            out_copy(c, which).wait()

    def step(it, carry):
        @pl.when(it + AHEAD < chunks)
        def _():
            send_own(it + AHEAD)

        @pl.when(it < chunks)
        def _():
            gather(it)
            attend(it)

        right_chunk = it - me
        left_chunk = it - (last - me)

        for hop in range(last, 0, -1):

            @pl.when((me + hop <= last) & (right_chunk >= 0) & (right_chunk < chunks))
            def _():
                relay(SUM_RIGHT, from_left, right_chunk, me + hop, has_left)

            @pl.when((me - hop >= 0) & (left_chunk >= 0) & (left_chunk < chunks))
            def _():
                relay(SUM_LEFT, from_right, left_chunk, me - hop, has_right)

        @pl.when(it >= last)
        def _():
            finish(it - last)

        return carry

    lax.fori_loop(0, chunks + last, step, 0)

    def drain(c, carry):
        for which in range(2):
            sum_copy(c, which).wait()
        return carry

    lax.fori_loop(0, chunks, drain, 0)


def on_device(
    queries, resp_keys, resp_values, grad_out, prefix_keys, prefix_values, block_mask, lengths
):
    rows, features = queries.shape
    span = prefix_keys.shape[0]
    groups = lax.axis_size("resp")
    chunks = features // WIDTH
    anywhere = pl.BlockSpec(memory_space=pl.ANY)
    scalars = pl.BlockSpec(memory_space=pltpu.SMEM)
    shared = (chunks, groups, 2, span, WIDTH)
    per_row = jax.ShapeDtypeStruct(queries.shape, jnp.bfloat16)
    per_prefix = jax.ShapeDtypeStruct(prefix_keys.shape, jnp.bfloat16)
    keys = groups * span + rows
    return pl.pallas_call(
        functools.partial(kernel, groups),
        out_shape=(per_row,) * 4 + (per_prefix,) * 2,
        in_specs=[scalars] * 2 + [anywhere] * 6,
        out_specs=(anywhere,) * 6,
        scratch_shapes=[
            pltpu.VMEM(shared, jnp.bfloat16),
            pltpu.VMEM((4, chunks, rows, WIDTH), jnp.bfloat16),
            pltpu.VMEM((4, chunks, rows, WIDTH), jnp.bfloat16),
            pltpu.VMEM(shared, jnp.bfloat16),
            pltpu.VMEM(shared, jnp.bfloat16),
            pltpu.VMEM(shared, jnp.bfloat16),
            pltpu.VMEM((chunks, 2, span, WIDTH), jnp.bfloat16),
            pltpu.VMEM((2, span, WIDTH), jnp.float32),
            pltpu.VMEM((rows, keys), jnp.int32),
            pltpu.SemaphoreType.DMA((4, chunks, groups)),
            pltpu.SemaphoreType.DMA((4, chunks, groups)),
            pltpu.SemaphoreType.DMA((chunks, 2)),
            pltpu.SemaphoreType.DMA((chunks, 4)),
            pltpu.SemaphoreType.DMA((chunks, 4)),
            pltpu.SemaphoreType.DMA((chunks, 2)),
        ],
        compiler_params=pltpu.CompilerParams(
            collective_id=0, has_side_effects=True, vmem_limit_bytes=56 * 2**20
        ),
        cost_estimate=pl.CostEstimate(
            flops=12 * rows * keys * features,
            bytes_accessed=10 * rows * features * 2,
            transcendentals=rows * keys * features // HD,
        ),
        name="shared_prompt_attention",
    )(
        block_mask,
        lengths,
        queries,
        resp_keys,
        resp_values,
        grad_out,
        prefix_keys,
        prefix_values,
    )


def solution(mesh):
    rows = P(("prompt", "resp"), None)
    return jax.shard_map(
        on_device,
        mesh=mesh,
        in_specs=(rows,) * 7 + (P(("prompt", "resp")),),
        out_specs=(rows,) * 6,
        check_vma=False,
    )
```

```python
import functools

import jax
import jax.numpy as jnp
from jax import lax
from jax.experimental import pallas as pl
from jax.experimental.pallas import tpu as pltpu
from jax.sharding import PartitionSpec as P

HD = 128
BLK = 128
WIDTH = 512
AHEAD = 2
LAG = 2
MESH = pl.DeviceIdType.MESH

GATHER_RIGHT, GATHER_LEFT, SUM_RIGHT, SUM_LEFT = 0, 1, 2, 3


def kernel(
    groups,
    mask_ref,
    length_ref,
    q_hbm,
    k_hbm,
    v_hbm,
    g_hbm,
    pk_hbm,
    pv_hbm,
    att_hbm,
    gq_hbm,
    gk_hbm,
    gv_hbm,
    gpk_hbm,
    gpv_hbm,
    kv,
    ins,
    outs,
    term,
    from_left,
    from_right,
    summed,
    total,
    visible,
    send_sem,
    recv_sem,
    prefix_sem,
    in_sem,
    out_sem,
    sum_sem,
):
    me = lax.axis_index("resp")
    chunks, _, _, span, width = kv.shape
    rows = ins.shape[2]
    prefix = groups * span
    last = groups - 1
    has_left = me > 0
    has_right = me < last

    def columns(c):
        return pl.ds(pl.multiple_of(c * width, width), width)

    def prefix_copy(c, which):
        source = (pk_hbm, pv_hbm)[which]
        return pltpu.make_async_copy(
            source.at[:, columns(c)], kv.at[c, me, which], prefix_sem.at[c, which]
        )

    def in_copy(c, which):
        source = (q_hbm, k_hbm, v_hbm, g_hbm)[which]
        return pltpu.make_async_copy(
            source.at[:, columns(c)], ins.at[which, c], in_sem.at[c, which]
        )

    def out_copy(c, which):
        target = (att_hbm, gq_hbm, gk_hbm, gv_hbm)[which]
        return pltpu.make_async_copy(
            outs.at[which, c], target.at[:, columns(c)], out_sem.at[c, which]
        )

    def sum_copy(c, which):
        target = (gpk_hbm, gpv_hbm)[which]
        return pltpu.make_async_copy(
            summed.at[c, which], target.at[:, columns(c)], sum_sem.at[c, which]
        )

    def remote(kind, c, slot):
        buffer = (kv, kv, from_left, from_right)[kind]
        to = me + 1 if kind in (GATHER_RIGHT, SUM_RIGHT) else me - 1
        return pltpu.make_async_remote_copy(
            src_ref=buffer.at[c, slot],
            dst_ref=buffer.at[c, slot],
            send_sem=send_sem.at[kind, c, slot],
            recv_sem=recv_sem.at[kind, c, slot],
            device_id={"resp": to},
            device_id_type=MESH,
        )

    def send_own(c):
        for which in range(2):
            prefix_copy(c, which).wait()

        @pl.when(has_right)
        def _():
            remote(GATHER_RIGHT, c, me).start()

        @pl.when(has_left)
        def _():
            remote(GATHER_LEFT, c, me).start()

    def start_prefix(c, carry):
        for which in range(2):
            prefix_copy(c, which).start()
        return carry

    def start_ins(c, carry):
        for which in range(4):
            in_copy(c, which).start()
        return carry

    lax.fori_loop(0, chunks, start_prefix, 0)
    barrier = pltpu.get_barrier_semaphore()

    @pl.when(has_left)
    def _():
        pl.semaphore_signal(barrier, inc=1, device_id={"resp": me - 1}, device_id_type=MESH)

    @pl.when(has_right)
    def _():
        pl.semaphore_signal(barrier, inc=1, device_id={"resp": me + 1}, device_id_type=MESH)

    @pl.when(has_left & has_right)
    def _():
        pl.semaphore_wait(barrier, 2)

    @pl.when(jnp.logical_not(has_left & has_right))
    def _():
        pl.semaphore_wait(barrier, 1)

    for c in range(AHEAD):
        send_own(c)
    lax.fori_loop(0, chunks, start_ins, 0)

    key_at = lax.broadcasted_iota(jnp.int32, (rows, prefix + rows), 1)
    row_at = lax.broadcasted_iota(jnp.int32, (rows, prefix + rows), 0)
    seen = jnp.where(key_at - prefix <= row_at, 1, 0)
    for block in range(prefix // BLK):
        inside = (key_at >= block * BLK) & (key_at < (block + 1) * BLK)
        seen = jnp.where(inside, mask_ref[0, block], seen)
    visible[...] = seen
    scaling = 1.0 / HD**0.5

    def gather(c):
        for hop in range(1, groups):

            @pl.when(me - hop >= 0)
            def _():
                remote(GATHER_RIGHT, c, me - hop).wait_recv()

                @pl.when(has_right)
                def _():
                    remote(GATHER_RIGHT, c, me - hop).start()

            @pl.when(me + hop <= last)
            def _():
                remote(GATHER_LEFT, c, me + hop).wait_recv()

                @pl.when(has_left)
                def _():
                    remote(GATHER_LEFT, c, me + hop).start()

    def attend(c):
        for which in range(4):
            in_copy(c, which).wait()
        valid = lax.broadcasted_iota(jnp.int32, (rows, HD), 0) < length_ref[0]
        for head in range(width // HD):
            at = slice(head * HD, (head + 1) * HD)
            query = ins[0, c, :, at]
            keys = jnp.concatenate(
                [kv[c, :, 0, :, at].reshape(prefix, HD), ins[1, c, :, at]], axis=0
            )
            values = jnp.concatenate(
                [kv[c, :, 1, :, at].reshape(prefix, HD), ins[2, c, :, at]], axis=0
            )
            grad32 = jnp.where(valid, ins[3, c, :, at].astype(jnp.float32), 0.0)
            grad = grad32.astype(jnp.bfloat16)
            across = (((1,), (1,)), ((), ()))
            down = (((0,), (0,)), ((), ()))
            scores = (
                lax.dot_general(query, keys, across, preferred_element_type=jnp.float32) * scaling
            )
            scores = jnp.where(visible[...] > 0, scores, -jnp.inf)
            powers = jnp.exp(scores - jnp.max(scores, axis=1, keepdims=True))
            probs = powers * (1.0 / jnp.sum(powers, axis=1, keepdims=True))
            weights = probs.astype(jnp.bfloat16)
            attended = jnp.dot(weights, values, preferred_element_type=jnp.float32).astype(
                jnp.bfloat16
            )
            outs[0, c, :, at] = attended
            delta = jnp.sum(grad32 * attended.astype(jnp.float32), axis=1, keepdims=True)
            dprob = lax.dot_general(grad, values, across, preferred_element_type=jnp.float32)
            dscore = (probs * (dprob - delta)).astype(jnp.bfloat16)
            grad_query = jnp.dot(dscore, keys, preferred_element_type=jnp.float32) * scaling
            outs[1, c, :, at] = grad_query.astype(jnp.bfloat16)
            grad_key = (
                lax.dot_general(dscore, query, down, preferred_element_type=jnp.float32) * scaling
            ).astype(jnp.bfloat16)
            grad_value = lax.dot_general(
                weights, grad, down, preferred_element_type=jnp.float32
            ).astype(jnp.bfloat16)
            term[c, :, 0, :, at] = grad_key[:prefix].reshape(groups, span, HD)
            term[c, :, 1, :, at] = grad_value[:prefix].reshape(groups, span, HD)
            outs[2, c, :, at] = grad_key[prefix:]
            outs[3, c, :, at] = grad_value[prefix:]
        for which in range(4):
            out_copy(c, which).start()

    def relay(kind, buffer, c, slot, receives):
        @pl.when(receives)
        def _():
            remote(kind, c, slot).wait_recv()
            buffer[c, slot] = (
                buffer[c, slot].astype(jnp.float32) + term[c, slot].astype(jnp.float32)
            ).astype(jnp.bfloat16)

        @pl.when(jnp.logical_not(receives))
        def _():
            buffer[c, slot] = term[c, slot]

        remote(kind, c, slot).start()

    def finish(c):
        total[...] = term[c, me].astype(jnp.float32)

        @pl.when(has_left)
        def _():
            remote(SUM_RIGHT, c, me).wait_recv()
            total[...] += from_left[c, me].astype(jnp.float32)

        @pl.when(has_right)
        def _():
            remote(SUM_LEFT, c, me).wait_recv()
            total[...] += from_right[c, me].astype(jnp.float32)

        summed[c] = total[...].astype(jnp.bfloat16)
        for which in range(2):
            sum_copy(c, which).start()
        for hop in range(groups):

            @pl.when((me - hop >= 0) & has_right)
            def _():
                remote(GATHER_RIGHT, c, me - hop).wait_send()

            @pl.when((me + hop <= last) & has_left)
            def _():
                remote(GATHER_LEFT, c, me + hop).wait_send()

            if hop > 0:

                @pl.when(me + hop <= last)
                def _():
                    remote(SUM_RIGHT, c, me + hop).wait_send()

                @pl.when(me - hop >= 0)
                def _():
                    remote(SUM_LEFT, c, me - hop).wait_send()

        for which in range(4):
            out_copy(c, which).wait()

    def step(it, carry):
        @pl.when(it + AHEAD < chunks)
        def _():
            send_own(it + AHEAD)

        @pl.when(it < chunks)
        def _():
            gather(it)
            attend(it)

        right_chunk = it - LAG * me
        left_chunk = it - LAG * (last - me)

        for hop in range(last, 0, -1):

            @pl.when((me + hop <= last) & (right_chunk >= 0) & (right_chunk < chunks))
            def _():
                relay(SUM_RIGHT, from_left, right_chunk, me + hop, has_left)

            @pl.when((me - hop >= 0) & (left_chunk >= 0) & (left_chunk < chunks))
            def _():
                relay(SUM_LEFT, from_right, left_chunk, me - hop, has_right)

        @pl.when(it >= LAG * last)
        def _():
            finish(it - LAG * last)

        return carry

    lax.fori_loop(0, chunks + LAG * last, step, 0)

    def drain(c, carry):
        for which in range(2):
            sum_copy(c, which).wait()
        return carry

    lax.fori_loop(0, chunks, drain, 0)


def hand_over(*refs):
    for source, target in zip(refs[:6], refs[6:]):
        target[...] = source[...]


def on_device(
    queries, resp_keys, resp_values, grad_out, prefix_keys, prefix_values, block_mask, lengths
):
    rows, features = queries.shape
    span = prefix_keys.shape[0]
    groups = lax.axis_size("resp")
    chunks = features // WIDTH
    anywhere = pl.BlockSpec(memory_space=pl.ANY)
    scalars = pl.BlockSpec(memory_space=pltpu.SMEM)
    shared = (chunks, groups, 2, span, WIDTH)
    per_row = jax.ShapeDtypeStruct(queries.shape, jnp.bfloat16)
    per_prefix = jax.ShapeDtypeStruct(prefix_keys.shape, jnp.bfloat16)
    keys = groups * span + rows
    results = pl.pallas_call(
        functools.partial(kernel, groups),
        out_shape=(per_row,) * 4 + (per_prefix,) * 2,
        in_specs=[scalars] * 2 + [anywhere] * 6,
        out_specs=(anywhere,) * 6,
        scratch_shapes=[
            pltpu.VMEM(shared, jnp.bfloat16),
            pltpu.VMEM((4, chunks, rows, WIDTH), jnp.bfloat16),
            pltpu.VMEM((4, chunks, rows, WIDTH), jnp.bfloat16),
            pltpu.VMEM(shared, jnp.bfloat16),
            pltpu.VMEM(shared, jnp.bfloat16),
            pltpu.VMEM(shared, jnp.bfloat16),
            pltpu.VMEM((chunks, 2, span, WIDTH), jnp.bfloat16),
            pltpu.VMEM((2, span, WIDTH), jnp.float32),
            pltpu.VMEM((rows, keys), jnp.int32),
            pltpu.SemaphoreType.DMA((4, chunks, groups)),
            pltpu.SemaphoreType.DMA((4, chunks, groups)),
            pltpu.SemaphoreType.DMA((chunks, 2)),
            pltpu.SemaphoreType.DMA((chunks, 4)),
            pltpu.SemaphoreType.DMA((chunks, 4)),
            pltpu.SemaphoreType.DMA((chunks, 2)),
        ],
        compiler_params=pltpu.CompilerParams(
            collective_id=0, has_side_effects=True, vmem_limit_bytes=56 * 2**20
        ),
        cost_estimate=pl.CostEstimate(
            flops=12 * rows * keys * features,
            bytes_accessed=10 * rows * features * 2,
            transcendentals=rows * keys * features // HD,
        ),
        name="shared_prompt_attention",
    )(
        block_mask,
        lengths,
        queries,
        resp_keys,
        resp_values,
        grad_out,
        prefix_keys,
        prefix_values,
    )
    pieces = 4
    blocks = [
        pl.BlockSpec((result.shape[0] // pieces, features), lambda at: (at, 0))
        for result in results
    ]
    return pl.pallas_call(
        hand_over,
        grid=(pieces,),
        out_shape=(per_row,) * 4 + (per_prefix,) * 2,
        in_specs=blocks,
        out_specs=tuple(blocks),
        compiler_params=pltpu.CompilerParams(vmem_limit_bytes=56 * 2**20),
        name="hand_over",
    )(*results)


def solution(mesh):
    rows = P(("prompt", "resp"), None)
    return jax.shard_map(
        on_device,
        mesh=mesh,
        in_specs=(rows,) * 7 + (P(("prompt", "resp")),),
        out_specs=(rows,) * 6,
        check_vma=False,
    )
```

```python
import functools

import jax
import jax.numpy as jnp
from jax import lax
from jax.experimental import pallas as pl
from jax.experimental.pallas import tpu as pltpu
from jax.sharding import PartitionSpec as P

HD = 128
BLK = 128
WIDTH = 512
AHEAD = 2
MESH = pl.DeviceIdType.MESH

GATHER_RIGHT, GATHER_LEFT, SUM_RIGHT, SUM_LEFT = 0, 1, 2, 3


def kernel(
    groups,
    mask_ref,
    length_ref,
    q_hbm,
    k_hbm,
    v_hbm,
    g_hbm,
    pk_hbm,
    pv_hbm,
    att_hbm,
    gq_hbm,
    gk_hbm,
    gv_hbm,
    gpk_hbm,
    gpv_hbm,
    kv,
    ins,
    outs,
    term,
    from_left,
    from_right,
    summed,
    total,
    visible,
    send_sem,
    recv_sem,
    prefix_sem,
    in_sem,
    out_sem,
    sum_sem,
):
    me = lax.axis_index("resp")
    chunks, _, _, span, width = kv.shape
    rows = ins.shape[2]
    prefix = groups * span
    last = groups - 1
    has_left = me > 0
    has_right = me < last

    def columns(c):
        return pl.ds(pl.multiple_of(c * width, width), width)

    def prefix_copy(c, which):
        source = (pk_hbm, pv_hbm)[which]
        return pltpu.make_async_copy(
            source.at[:, columns(c)], kv.at[c, me, which], prefix_sem.at[c, which]
        )

    def in_copy(c, which):
        source = (q_hbm, k_hbm, v_hbm, g_hbm)[which]
        return pltpu.make_async_copy(
            source.at[:, columns(c)], ins.at[which, c], in_sem.at[c, which]
        )

    def out_copy(c, which):
        target = (att_hbm, gq_hbm, gk_hbm, gv_hbm)[which]
        return pltpu.make_async_copy(
            outs.at[which, c], target.at[:, columns(c)], out_sem.at[c, which]
        )

    def sum_copy(c, which):
        target = (gpk_hbm, gpv_hbm)[which]
        return pltpu.make_async_copy(
            summed.at[c, which], target.at[:, columns(c)], sum_sem.at[c, which]
        )

    def remote(kind, c, slot):
        buffer = (kv, kv, from_left, from_right)[kind]
        to = me + 1 if kind in (GATHER_RIGHT, SUM_RIGHT) else me - 1
        return pltpu.make_async_remote_copy(
            src_ref=buffer.at[c, slot],
            dst_ref=buffer.at[c, slot],
            send_sem=send_sem.at[kind, c, slot],
            recv_sem=recv_sem.at[kind, c, slot],
            device_id={"resp": to},
            device_id_type=MESH,
        )

    def send_own(c):
        for which in range(2):
            prefix_copy(c, which).wait()

        @pl.when(has_right)
        def _():
            remote(GATHER_RIGHT, c, me).start()

        @pl.when(has_left)
        def _():
            remote(GATHER_LEFT, c, me).start()

    def start_prefix(c, carry):
        for which in range(2):
            prefix_copy(c, which).start()
        return carry

    def start_ins(c, carry):
        for which in range(4):
            in_copy(c, which).start()
        return carry

    lax.fori_loop(0, chunks, start_prefix, 0)
    barrier = pltpu.get_barrier_semaphore()

    @pl.when(has_left)
    def _():
        pl.semaphore_signal(barrier, inc=1, device_id={"resp": me - 1}, device_id_type=MESH)

    @pl.when(has_right)
    def _():
        pl.semaphore_signal(barrier, inc=1, device_id={"resp": me + 1}, device_id_type=MESH)

    @pl.when(has_left & has_right)
    def _():
        pl.semaphore_wait(barrier, 2)

    @pl.when(jnp.logical_not(has_left & has_right))
    def _():
        pl.semaphore_wait(barrier, 1)

    for c in range(AHEAD):
        send_own(c)
    lax.fori_loop(0, chunks, start_ins, 0)

    key_at = lax.broadcasted_iota(jnp.int32, (rows, prefix + rows), 1)
    row_at = lax.broadcasted_iota(jnp.int32, (rows, prefix + rows), 0)
    seen = jnp.where(key_at - prefix <= row_at, 1, 0)
    for block in range(prefix // BLK):
        inside = (key_at >= block * BLK) & (key_at < (block + 1) * BLK)
        seen = jnp.where(inside, mask_ref[0, block], seen)
    visible[...] = seen
    scaling = 1.0 / HD**0.5

    def gather(c):
        for hop in range(1, groups):

            @pl.when(me - hop >= 0)
            def _():
                remote(GATHER_RIGHT, c, me - hop).wait_recv()

                @pl.when(has_right)
                def _():
                    remote(GATHER_RIGHT, c, me - hop).start()

            @pl.when(me + hop <= last)
            def _():
                remote(GATHER_LEFT, c, me + hop).wait_recv()

                @pl.when(has_left)
                def _():
                    remote(GATHER_LEFT, c, me + hop).start()

    def attend(c):
        for which in range(4):
            in_copy(c, which).wait()
        valid = lax.broadcasted_iota(jnp.int32, (rows, HD), 0) < length_ref[0]
        for head in range(width // HD):
            at = slice(head * HD, (head + 1) * HD)
            query = ins[0, c, :, at]
            keys = jnp.concatenate(
                [kv[c, :, 0, :, at].reshape(prefix, HD), ins[1, c, :, at]], axis=0
            )
            values = jnp.concatenate(
                [kv[c, :, 1, :, at].reshape(prefix, HD), ins[2, c, :, at]], axis=0
            )
            grad32 = jnp.where(valid, ins[3, c, :, at].astype(jnp.float32), 0.0)
            grad = grad32.astype(jnp.bfloat16)
            across = (((1,), (1,)), ((), ()))
            down = (((0,), (0,)), ((), ()))
            scores = (
                lax.dot_general(query, keys, across, preferred_element_type=jnp.float32) * scaling
            )
            scores = jnp.where(visible[...] > 0, scores, -jnp.inf)
            powers = jnp.exp(scores - jnp.max(scores, axis=1, keepdims=True))
            probs = powers * (1.0 / jnp.sum(powers, axis=1, keepdims=True))
            weights = probs.astype(jnp.bfloat16)
            attended = jnp.dot(weights, values, preferred_element_type=jnp.float32).astype(
                jnp.bfloat16
            )
            outs[0, c, :, at] = attended
            delta = jnp.sum(grad32 * attended.astype(jnp.float32), axis=1, keepdims=True)
            dprob = lax.dot_general(grad, values, across, preferred_element_type=jnp.float32)
            dscore = (probs * (dprob - delta)).astype(jnp.bfloat16)
            grad_query = jnp.dot(dscore, keys, preferred_element_type=jnp.float32) * scaling
            outs[1, c, :, at] = grad_query.astype(jnp.bfloat16)
            grad_key = (
                lax.dot_general(dscore, query, down, preferred_element_type=jnp.float32) * scaling
            ).astype(jnp.bfloat16)
            grad_value = lax.dot_general(
                weights, grad, down, preferred_element_type=jnp.float32
            ).astype(jnp.bfloat16)
            term[c, :, 0, :, at] = grad_key[:prefix].reshape(groups, span, HD)
            term[c, :, 1, :, at] = grad_value[:prefix].reshape(groups, span, HD)
            outs[2, c, :, at] = grad_key[prefix:]
            outs[3, c, :, at] = grad_value[prefix:]
        for which in range(4):
            out_copy(c, which).start()

    def relay(kind, buffer, c, slot, receives):
        @pl.when(receives)
        def _():
            remote(kind, c, slot).wait_recv()
            buffer[c, slot] = (
                buffer[c, slot].astype(jnp.float32) + term[c, slot].astype(jnp.float32)
            ).astype(jnp.bfloat16)

        @pl.when(jnp.logical_not(receives))
        def _():
            buffer[c, slot] = term[c, slot]

        remote(kind, c, slot).start()

    def finish(c):
        total[...] = term[c, me].astype(jnp.float32)

        @pl.when(has_left)
        def _():
            remote(SUM_RIGHT, c, me).wait_recv()
            total[...] += from_left[c, me].astype(jnp.float32)

        @pl.when(has_right)
        def _():
            remote(SUM_LEFT, c, me).wait_recv()
            total[...] += from_right[c, me].astype(jnp.float32)

        summed[c] = total[...].astype(jnp.bfloat16)
        for which in range(2):
            sum_copy(c, which).start()
        for hop in range(groups):

            @pl.when((me - hop >= 0) & has_right)
            def _():
                remote(GATHER_RIGHT, c, me - hop).wait_send()

            @pl.when((me + hop <= last) & has_left)
            def _():
                remote(GATHER_LEFT, c, me + hop).wait_send()

            if hop > 0:

                @pl.when(me + hop <= last)
                def _():
                    remote(SUM_RIGHT, c, me + hop).wait_send()

                @pl.when(me - hop >= 0)
                def _():
                    remote(SUM_LEFT, c, me - hop).wait_send()

        for which in range(4):
            out_copy(c, which).wait()

    def step(it, carry):
        @pl.when(it + AHEAD < chunks)
        def _():
            send_own(it + AHEAD)

        @pl.when(it < chunks)
        def _():
            gather(it)
            attend(it)

        right_chunk = it - me - jnp.where(me > 0, 1, 0)
        left_chunk = it - (last - me) - jnp.where(me < last, 1, 0)

        for hop in range(last, 0, -1):

            @pl.when((me + hop <= last) & (right_chunk >= 0) & (right_chunk < chunks))
            def _():
                relay(SUM_RIGHT, from_left, right_chunk, me + hop, has_left)

            @pl.when((me - hop >= 0) & (left_chunk >= 0) & (left_chunk < chunks))
            def _():
                relay(SUM_LEFT, from_right, left_chunk, me - hop, has_right)

        @pl.when(it >= (last + 1))
        def _():
            finish(it - (last + 1))

        return carry

    lax.fori_loop(0, chunks + (last + 1), step, 0)

    def drain(c, carry):
        for which in range(2):
            sum_copy(c, which).wait()
        return carry

    lax.fori_loop(0, chunks, drain, 0)


def hand_over(*refs):
    for source, target in zip(refs[:6], refs[6:]):
        target[...] = source[...]


def on_device(
    queries, resp_keys, resp_values, grad_out, prefix_keys, prefix_values, block_mask, lengths
):
    rows, features = queries.shape
    span = prefix_keys.shape[0]
    groups = lax.axis_size("resp")
    chunks = features // WIDTH
    anywhere = pl.BlockSpec(memory_space=pl.ANY)
    scalars = pl.BlockSpec(memory_space=pltpu.SMEM)
    shared = (chunks, groups, 2, span, WIDTH)
    per_row = jax.ShapeDtypeStruct(queries.shape, jnp.bfloat16)
    per_prefix = jax.ShapeDtypeStruct(prefix_keys.shape, jnp.bfloat16)
    keys = groups * span + rows
    results = pl.pallas_call(
        functools.partial(kernel, groups),
        out_shape=(per_row,) * 4 + (per_prefix,) * 2,
        in_specs=[scalars] * 2 + [anywhere] * 6,
        out_specs=(anywhere,) * 6,
        scratch_shapes=[
            pltpu.VMEM(shared, jnp.bfloat16),
            pltpu.VMEM((4, chunks, rows, WIDTH), jnp.bfloat16),
            pltpu.VMEM((4, chunks, rows, WIDTH), jnp.bfloat16),
            pltpu.VMEM(shared, jnp.bfloat16),
            pltpu.VMEM(shared, jnp.bfloat16),
            pltpu.VMEM(shared, jnp.bfloat16),
            pltpu.VMEM((chunks, 2, span, WIDTH), jnp.bfloat16),
            pltpu.VMEM((2, span, WIDTH), jnp.float32),
            pltpu.VMEM((rows, keys), jnp.int32),
            pltpu.SemaphoreType.DMA((4, chunks, groups)),
            pltpu.SemaphoreType.DMA((4, chunks, groups)),
            pltpu.SemaphoreType.DMA((chunks, 2)),
            pltpu.SemaphoreType.DMA((chunks, 4)),
            pltpu.SemaphoreType.DMA((chunks, 4)),
            pltpu.SemaphoreType.DMA((chunks, 2)),
        ],
        compiler_params=pltpu.CompilerParams(
            collective_id=0, has_side_effects=True, vmem_limit_bytes=56 * 2**20
        ),
        cost_estimate=pl.CostEstimate(
            flops=12 * rows * keys * features,
            bytes_accessed=10 * rows * features * 2,
            transcendentals=rows * keys * features // HD,
        ),
        name="shared_prompt_attention",
    )(
        block_mask,
        lengths,
        queries,
        resp_keys,
        resp_values,
        grad_out,
        prefix_keys,
        prefix_values,
    )
    pieces = 4
    blocks = [
        pl.BlockSpec((result.shape[0] // pieces, features), lambda at: (at, 0))
        for result in results
    ]
    return pl.pallas_call(
        hand_over,
        grid=(pieces,),
        out_shape=(per_row,) * 4 + (per_prefix,) * 2,
        in_specs=blocks,
        out_specs=tuple(blocks),
        compiler_params=pltpu.CompilerParams(vmem_limit_bytes=56 * 2**20),
        name="hand_over",
    )(*results)


def solution(mesh):
    rows = P(("prompt", "resp"), None)
    return jax.shard_map(
        on_device,
        mesh=mesh,
        in_specs=(rows,) * 7 + (P(("prompt", "resp")),),
        out_specs=(rows,) * 6,
        check_vma=False,
    )
```
